32 devices in a mesh: occ: 8 (over y, x, core), vir: 4 (over z).
Axes of the slice: x: 2, y: 2, z: 4, core: 2. Of those that a mesh axis runs over, the one named last changes fastest.
Arguments:
- amplitudes: bfloat16 [1600, 2560], P('occ', 'vir'), may hold values from -6 to 6
- ladder_ints: bfloat16 [2560, 2560], P('vir', 'occ'), may hold values from -0.15625 to 0.15625
- cycle_ints: bfloat16 [2560, 2560], P('vir', 'occ'), may hold values from -0.15625 to 0.15625
- screen: int32 [40, 40], P('occ', 'vir'), may hold values 0 or 1
Outputs:
- residual: bfloat16 [1600, 2560], P('occ', 'vir')
The draws below stay inside these ranges and needn't reach their ends.
All inputs are finite; a program needn't handle non-finite values. No bound on the sum of `screen` on one device may be relied on, other than what follows from the above.
Results may differ from the reference program's by a relative error of at most 0.0044.
Values may be sent and summed in bfloat16 or wider, within the bound.
A program may use at most 128 MiB of HBM per device.

```python
import jax
import jax.numpy as jnp

TILE = 64
NOCC = 40
VPT = 40
VP = 2560
OPAIRS = 1600


def touch_ends(result, rng, low, largest):
    spot = [jax.random.randint(jax.random.fold_in(rng, axis), (), 0, length) for axis, length in enumerate(result.shape)]
    widest = result.shape.index(max(result.shape))
    beside = spot[:widest] + [(spot[widest] + 1) % result.shape[widest]] + spot[widest + 1:]
    return result.at[tuple(spot)].set(low).at[tuple(beside)].set(largest)


def strengthened(result, stream_key, source, target, shards_of, factor):
    owner, partner = [(jnp.arange(result.shape[axis_at]) // (result.shape[axis_at] // shards_of)).reshape([-1 if axis == axis_at else 1 for axis in range(result.ndim)]) for axis_at in (source, target)]
    chosen = jax.random.permutation(stream_key, shards_of)[partner]
    strong = (owner == chosen) | (owner == (partner + shards_of // 2) % shards_of)
    return jnp.where(strong, factor * result, result)


def block_scale(rng, extent, cuts, smallest, largest):
    loudness = 1.0
    for axis_at, shards_of in cuts:
        heights = jax.random.uniform(jax.random.fold_in(jax.random.fold_in(rng, 6), axis_at), (shards_of,), jnp.float32, smallest / len(cuts), largest / len(cuts))
        loudness = loudness * jnp.repeat(jnp.exp(heights), extent[axis_at] // shards_of).reshape((-1,) + (1,) * (len(extent) - 1 - axis_at))
    return loudness


def scatter_about(rng, extent, deviation, bound, split=(), held_as=jnp.bfloat16):
    gain = block_scale(rng, extent, split, -0.22, 0.18) if split else 1.0
    drawn = jax.random.normal(rng, extent, jnp.float32) * deviation * gain
    return jnp.minimum(jnp.maximum(drawn, -bound), bound).astype(held_as)


def gaussian_with(own_key, dims, width, limit, pieces, heavy, held_as=jnp.bfloat16):
    result = width * jax.random.normal(own_key, dims, jnp.float32)
    if pieces:
        result = result * block_scale(own_key, dims, pieces, -0.22, 0.18)
    return jnp.clip(strengthened(result, jax.random.fold_in(own_key, 3), *heavy), -limit, limit).astype(held_as)


def setup_inputs(seed: int = 0) -> dict:
    key_list = jax.random.split(jax.random.key(seed), 5)
    return {
        "amplitudes": scatter_about(key_list[0], (OPAIRS, VP), 1.0, 6.0, ((0, 8), (1, 4))),
        "ladder_ints": gaussian_with(key_list[1], (VP, VP), VP ** -0.5, 0.15625, ((0, 4), (1, 8)), (0, 1, 8, 2.0)),
        "cycle_ints": gaussian_with(key_list[2], (VP, VP), VP ** -0.5, 0.15625, ((0, 4), (1, 8)), (0, 1, 8, 2.0)),
        "screen": touch_ends((jax.random.randint(key_list[3], (NOCC, VPT), 0, 4) < 3).astype(jnp.int32), jax.random.fold_in(key_list[3], 1), 0, 1),
    }


def expand_screen(screen):
    values = screen.astype(jnp.float32)
    spread = jnp.broadcast_to(values[:, None, :, None], (NOCC, NOCC, VPT, TILE))
    return spread.reshape(NOCC * NOCC, VP)


def reference(amplitudes, ladder_ints, cycle_ints, screen):
    keep = expand_screen(screen)
    masked = (amplitudes.astype(jnp.float32) * keep).astype(jnp.bfloat16)
    swapped = masked.reshape(NOCC, NOCC, VP).transpose(1, 0, 2).reshape(NOCC * NOCC, VP)
    cycle_input = (2.0 * masked.astype(jnp.float32) - swapped.astype(jnp.float32)).astype(jnp.bfloat16)
    ladder = jnp.dot(masked, ladder_ints, preferred_element_type=jnp.float32)
    cycle_part = jnp.dot(cycle_input, cycle_ints, preferred_element_type=jnp.float32)
    return (keep * (ladder + cycle_part)).astype(jnp.bfloat16)
```

```python
import functools

import jax
import jax.numpy as jnp
from jax import lax
from jax.experimental import pallas as pl
from jax.experimental.pallas import tpu as pltpu
from jax.sharding import PartitionSpec as P

MESH = pl.DeviceIdType.MESH
LANES = 128
F32, BF16 = jnp.float32, jnp.bfloat16


def plain(amplitudes, ladder_ints, cycle_ints, screen):
    orbital_rows, tile_count = screen.shape
    occupied = amplitudes.shape[0] // orbital_rows
    columns = amplitudes.shape[1]
    tile_width = columns // tile_count
    groups = lax.axis_size("occ")
    values = screen.astype(F32)
    keep = jnp.broadcast_to(
        values[:, None, :, None], (orbital_rows, occupied, tile_count, tile_width)
    )
    keep = keep.reshape(orbital_rows * occupied, columns)
    masked = (amplitudes.astype(F32) * keep).astype(BF16)
    blocks = masked.reshape(orbital_rows, groups, orbital_rows, columns)
    arrived = lax.all_to_all(blocks, "occ", split_axis=1, concat_axis=1, tiled=True)
    swapped = arrived.transpose(2, 1, 0, 3).reshape(orbital_rows * occupied, columns)
    cycle_input = (2.0 * masked.astype(F32) - swapped.astype(F32)).astype(BF16)
    cycle_part = jnp.dot(
        cycle_input,
        lax.all_gather(cycle_ints, "occ", axis=1, tiled=True),
        preferred_element_type=F32,
    )
    ladder = jnp.dot(
        masked,
        lax.all_gather(ladder_ints, "occ", axis=1, tiled=True),
        preferred_element_type=F32,
    )
    summed = lax.psum_scatter(ladder + cycle_part, "vir", scatter_dimension=1, tiled=True)
    return (keep * summed).astype(BF16)


def kernel(
    nv, norb, nocc,
    amp, lad, cyc, scr, out,
    G, G32, I, W, O, R, keep_ref,
    gs, gr, osem, orx,
):
    rows, cols = out.shape
    pad = G.shape[1]
    half = cols // 2
    tile = cols // scr.shape[1]
    cut = (rows // 32) * 16
    o = lax.axis_index("occ")
    z = lax.axis_index("vir")
    k = o % 2
    c = o // 2
    nc = nv
    sib = o + 1 - 2 * k
    cx = c + 1 - 2 * (c % 2)
    cy = c + 2 - 4 * ((c // 2) % 2)
    cd = cx + 2 - 4 * ((cx // 2) % 2)
    X, Y, D = 2 * cx + k, 2 * cy + k, 2 * cd + k
    mine = z == c

    barrier = pltpu.get_barrier_semaphore()
    for p in (sib, X, Y):
        pl.semaphore_signal(barrier, inc=1, device_id={"occ": p, "vir": z}, device_id_type=MESH)
    for q in range(nv):
        src = 2 * z + k

        @pl.when(jnp.logical_not((src == o) & (z == q)))
        def _():
            pl.semaphore_signal(
                barrier, inc=1, device_id={"occ": src, "vir": q}, device_id_type=MESH
            )

    t_of = lax.broadcasted_iota(jnp.int32, (scr.shape[1], cols), 0)
    v_of = lax.broadcasted_iota(jnp.int32, (scr.shape[1], cols), 1)
    spread = ((v_of >= t_of * tile) & (v_of < (t_of + 1) * tile)).astype(F32)
    wide = jnp.dot(scr[...].astype(F32), spread, preferred_element_type=F32)
    r_of = lax.broadcasted_iota(jnp.int32, (rows, norb), 0)
    a_of = lax.broadcasted_iota(jnp.int32, (rows, norb), 1)
    pick = ((r_of >= a_of * nocc) & (r_of < (a_of + 1) * nocc)).astype(F32)
    keep = jnp.dot(pick, wide, preferred_element_type=F32)
    keep_ref[...] = keep
    masked = amp[...].astype(F32) * keep
    masked = jnp.concatenate([masked, jnp.zeros((pad - rows, cols), F32)], axis=0)
    G[o] = masked.astype(BF16)

    pl.semaphore_wait(barrier, jnp.where(mine, 3 + nv - 1, 3 + nv))

    def cp(src, dst, sem, p):
        return pltpu.make_async_remote_copy(
            src_ref=src, dst_ref=dst, send_sem=gs.at[sem], recv_sem=gr.at[sem],
            device_id={"occ": p, "vir": z}, device_id_type=MESH,
        )

    def blk(s, h=None):
        if h is None:
            return G.at[s]
        return G.at[s, pl.ds(0, cut)] if h == 0 else G.at[s, pl.ds(cut, pad - cut)]

    def widen(s):
        val = G[s].astype(F32)[:rows]
        at = pl.multiple_of(s * rows, 8)
        for l in range(cols // LANES):
            G32[l, pl.ds(at, rows), :] = val[:, l * LANES:(l + 1) * LANES]

    sends = []

    def send(s, h, sem, p):
        d = cp(blk(s, h), blk(s, h), sem, p)
        d.start()
        sends.append(d)

    def arrive(s, h, sem):
        cp(blk(s, h), blk(s, h), sem, sib).wait_recv()

    send(o, 0, 0, X)
    send(o, 1, 3, Y)
    send(o, 1, 1, X)
    send(o, 0, 2, Y)
    send(o, None, 6, sib)
    for m, ref in enumerate((lad, cyc)):
        d = cp(ref, I.at[k, m], 10 + m, sib)
        d.start()
        sends.append(d)
        I[k, m] = ref[...]
    widen(o)
    arrive(X, 0, 0)
    send(X, 0, 4, Y)
    arrive(Y, 1, 3)
    send(Y, 1, 5, X)
    arrive(sib, None, 6)
    widen(sib)
    for m in range(2):
        cp(I.at[1 - k, m], I.at[1 - k, m], 10 + m, sib).wait_recv()
        W[m] = jnp.concatenate([I[0, m], I[1, m]], axis=1)
    SX, SY, SD = X + 1 - 2 * k, Y + 1 - 2 * k, D + 1 - 2 * k
    arrive(X, 1, 1)
    send(X, None, 7, sib)
    arrive(Y, 0, 2)
    send(Y, None, 8, sib)
    widen(X)
    widen(Y)
    arrive(SX, None, 7)
    widen(SX)
    arrive(SY, None, 8)
    widen(SY)
    arrive(D, 0, 4)
    arrive(D, 1, 5)
    send(D, None, 9, sib)
    widen(D)
    arrive(SD, None, 9)
    widen(SD)

    def out_copy(t, chip, slot, zz):
        return pltpu.make_async_remote_copy(
            src_ref=O.at[t], dst_ref=R.at[slot], send_sem=osem.at[t], recv_sem=orx.at[slot],
            device_id={"occ": 2 * chip + k, "vir": zz}, device_id_type=MESH,
        )

    def step(t, carry):
        chip = (c + t + 1) % nc
        dest = 2 * chip + k
        m = G[dest]
        parts = []
        for a in range(norb):
            i = dest * norb + a
            parts.append(jnp.concatenate(
                [G32[l, pl.ds(i, nocc, stride=nocc), :] for l in range(cols // LANES)], axis=1))
        parts.append(jnp.zeros((pad - rows, cols), F32))
        swapped = jnp.concatenate(parts, axis=0)
        ci = (2.0 * m.astype(F32) - swapped).astype(BF16)
        acc = jnp.dot(m, W[0], preferred_element_type=F32)
        acc = acc + jnp.dot(ci, W[1], preferred_element_type=F32)
        O[t] = acc.astype(BF16)
        here = (chip == c) & mine

        @pl.when(jnp.logical_not(here))
        def _():
            out_copy(t, chip, z, c).start()

        return carry

    lax.fori_loop(0, nc, step, 0)

    total = None
    for q in range(nv):
        own = mine & (z == q)

        @pl.when(own)
        def _():
            R[q] = O[nc - 1]

        @pl.when(jnp.logical_not(own))
        def _():
            out_copy(0, c, q, z).wait_recv()

        part = R[q].astype(F32)[:rows]
        total = part if total is None else total + part
    out[...] = (keep_ref[...] * total).astype(BF16)

    for d in sends:
        d.wait_send()
    for t in range(nc):
        if t < nc - 1:
            out_copy(t, c, z, c).wait_send()
        else:
            @pl.when(jnp.logical_not(mine))
            def _():
                out_copy(t, c, z, c).wait_send()


def fused(amplitudes, ladder_ints, cycle_ints, screen):
    norb, tiles = screen.shape
    rows, cols = amplitudes.shape
    nocc = rows // norb
    nv = lax.axis_size("vir")
    groups = lax.axis_size("occ")
    pad = -(-rows // 16) * 16
    vmem = pl.BlockSpec(memory_space=pltpu.VMEM)
    return pl.pallas_call(
        functools.partial(kernel, nv, norb, nocc),
        out_shape=jax.ShapeDtypeStruct((rows, cols), BF16),
        in_specs=[vmem] * 4,
        out_specs=vmem,
        scratch_shapes=[
            pltpu.VMEM((groups, pad, cols), BF16),
            pltpu.VMEM((cols // LANES, groups * rows, LANES), F32),
            pltpu.VMEM((2, 2) + ladder_ints.shape, BF16),
            pltpu.VMEM((2, cols, cols), BF16),
            pltpu.VMEM((nv, pad, cols), BF16),
            pltpu.VMEM((nv, pad, cols), BF16),
            pltpu.VMEM((rows, cols), F32),
            pltpu.SemaphoreType.DMA((12,)),
            pltpu.SemaphoreType.DMA((12,)),
            pltpu.SemaphoreType.DMA((nv,)),
            pltpu.SemaphoreType.DMA((nv,)),
        ],
        compiler_params=pltpu.CompilerParams(
            collective_id=0, has_side_effects=True, vmem_limit_bytes=48 * 2**20
        ),
    )(amplitudes, ladder_ints, cycle_ints, screen)


def shards(amplitudes, ladder_ints, cycle_ints, screen):
    groups, planes = lax.axis_size("occ"), lax.axis_size("vir")
    rows, cols = amplitudes.shape
    fits = (
        groups == 2 * planes
        and planes == 4
        and cols == 2 * ladder_ints.shape[1]
        and cols == ladder_ints.shape[0]
        and cols % LANES == 0
        and (rows // screen.shape[0]) % 8 == 0
        and groups * rows * cols * 6 < 24 * 2**20
    )
    return (fused if fits else plain)(amplitudes, ladder_ints, cycle_ints, screen)


def solution(mesh):
    placed = (P("occ", "vir"), P("vir", "occ"), P("vir", "occ"), P("occ", "vir"))
    return jax.shard_map(
        shards, mesh=mesh, in_specs=placed, out_specs=P("occ", "vir"), check_vma=False
    )
```

```python
import functools

import jax
import jax.numpy as jnp
from jax import lax
from jax.experimental import pallas as pl
from jax.experimental.pallas import tpu as pltpu
from jax.sharding import PartitionSpec as P

MESH = pl.DeviceIdType.MESH
LANES = 128
F32, BF16 = jnp.float32, jnp.bfloat16


def plain(amplitudes, ladder_ints, cycle_ints, screen):
    orbital_rows, tile_count = screen.shape
    occupied = amplitudes.shape[0] // orbital_rows
    columns = amplitudes.shape[1]
    tile_width = columns // tile_count
    groups = lax.axis_size("occ")
    values = screen.astype(F32)
    keep = jnp.broadcast_to(
        values[:, None, :, None], (orbital_rows, occupied, tile_count, tile_width)
    )
    keep = keep.reshape(orbital_rows * occupied, columns)
    masked = (amplitudes.astype(F32) * keep).astype(BF16)
    blocks = masked.reshape(orbital_rows, groups, orbital_rows, columns)
    arrived = lax.all_to_all(blocks, "occ", split_axis=1, concat_axis=1, tiled=True)
    swapped = arrived.transpose(2, 1, 0, 3).reshape(orbital_rows * occupied, columns)
    cycle_input = (2.0 * masked.astype(F32) - swapped.astype(F32)).astype(BF16)
    cycle_part = jnp.dot(
        cycle_input,
        lax.all_gather(cycle_ints, "occ", axis=1, tiled=True),
        preferred_element_type=F32,
    )
    ladder = jnp.dot(
        masked,
        lax.all_gather(ladder_ints, "occ", axis=1, tiled=True),
        preferred_element_type=F32,
    )
    summed = lax.psum_scatter(ladder + cycle_part, "vir", scatter_dimension=1, tiled=True)
    return (keep * summed).astype(BF16)


def kernel(
    nv, norb, nocc,
    amp, lad, cyc, scr, out,
    G, G32, I, W, O, T, R, keep_ref,
    gs, gr, osem, orx, lsem, lrx,
):
    rows, cols = out.shape
    pad = G.shape[1]
    half = cols // 2
    tile = cols // scr.shape[1]
    cut = (rows // 32) * 16
    o = lax.axis_index("occ")
    z = lax.axis_index("vir")
    k = o % 2
    c = o // 2
    nc = nv
    sib = o + 1 - 2 * k
    cx = c + 1 - 2 * (c % 2)
    cy = c + 2 - 4 * ((c // 2) % 2)
    cd = cx + 2 - 4 * ((cx // 2) % 2)
    X, Y, D = 2 * cx + k, 2 * cy + k, 2 * cd + k

    barrier = pltpu.get_barrier_semaphore()
    for p in (sib, X, Y, D):
        pl.semaphore_signal(barrier, inc=1, device_id={"occ": p, "vir": z}, device_id_type=MESH)
    for there, ok in ((z - 1, z > 0), (z + 1, z < nv - 1)):

        @pl.when(ok)
        def _():
            pl.semaphore_signal(
                barrier, inc=1, device_id={"occ": o, "vir": there}, device_id_type=MESH
            )

    t_of = lax.broadcasted_iota(jnp.int32, (scr.shape[1], cols), 0)
    v_of = lax.broadcasted_iota(jnp.int32, (scr.shape[1], cols), 1)
    spread = ((v_of >= t_of * tile) & (v_of < (t_of + 1) * tile)).astype(F32)
    wide = jnp.dot(scr[...].astype(F32), spread, preferred_element_type=F32)
    r_of = lax.broadcasted_iota(jnp.int32, (rows, norb), 0)
    a_of = lax.broadcasted_iota(jnp.int32, (rows, norb), 1)
    pick = ((r_of >= a_of * nocc) & (r_of < (a_of + 1) * nocc)).astype(F32)
    keep = jnp.dot(pick, wide, preferred_element_type=F32)
    keep_ref[...] = keep
    masked = amp[...].astype(F32) * keep
    masked = jnp.concatenate([masked, jnp.zeros((pad - rows, cols), F32)], axis=0)
    G[o] = masked.astype(BF16)

    pl.semaphore_wait(barrier, jnp.where((z == 0) | (z == nv - 1), 5, 6))

    def cp(src, dst, sem, p):
        return pltpu.make_async_remote_copy(
            src_ref=src, dst_ref=dst, send_sem=gs.at[sem], recv_sem=gr.at[sem],
            device_id={"occ": p, "vir": z}, device_id_type=MESH,
        )

    def blk(s, h=None):
        if h is None:
            return G.at[s]
        return G.at[s, pl.ds(0, cut)] if h == 0 else G.at[s, pl.ds(cut, pad - cut)]

    def widen(s):
        val = G[s].astype(F32)[:rows]
        at = pl.multiple_of(s * rows, 8)
        for l in range(cols // LANES):
            G32[l, pl.ds(at, rows), :] = val[:, l * LANES:(l + 1) * LANES]

    sends = []

    def send(s, h, sem, p):
        d = cp(blk(s, h), blk(s, h), sem, p)
        d.start()
        sends.append(d)

    def arrive(s, h, sem):
        cp(blk(s, h), blk(s, h), sem, sib).wait_recv()

    send(o, 0, 0, X)
    send(o, 1, 3, Y)
    send(o, 1, 1, X)
    send(o, 0, 2, Y)
    send(o, None, 6, sib)
    for m, ref in enumerate((lad, cyc)):
        d = cp(ref, I.at[k, m], 10 + m, sib)
        d.start()
        sends.append(d)
        I[k, m] = ref[...]
    widen(o)
    arrive(X, 0, 0)
    send(X, 0, 4, Y)
    arrive(Y, 1, 3)
    send(Y, 1, 5, X)
    arrive(sib, None, 6)
    widen(sib)
    for m in range(2):
        cp(I.at[1 - k, m], I.at[1 - k, m], 10 + m, sib).wait_recv()
        W[m] = jnp.concatenate([I[0, m], I[1, m]], axis=1)
    SX, SY, SD = X + 1 - 2 * k, Y + 1 - 2 * k, D + 1 - 2 * k
    arrive(X, 1, 1)
    send(X, None, 7, sib)
    arrive(Y, 0, 2)
    send(Y, None, 8, sib)
    widen(X)
    widen(Y)
    arrive(SX, None, 7)
    widen(SX)
    arrive(SY, None, 8)
    widen(SY)
    arrive(D, 0, 4)
    arrive(D, 1, 5)
    send(D, None, 9, sib)
    widen(D)
    arrive(SD, None, 9)
    widen(SD)

    def out_copy(t, chip, slot):
        return pltpu.make_async_remote_copy(
            src_ref=O.at[t], dst_ref=T.at[slot], send_sem=osem.at[t], recv_sem=orx.at[slot],
            device_id={"occ": 2 * chip + k, "vir": z}, device_id_type=MESH,
        )

    def step(t, carry):
        chip = (c + t + 1) % nc
        dest = 2 * chip + k
        m = G[dest]
        parts = []
        for a in range(norb):
            i = dest * norb + a
            parts.append(jnp.concatenate(
                [G32[l, pl.ds(i, nocc, stride=nocc), :] for l in range(cols // LANES)], axis=1))
        parts.append(jnp.zeros((pad - rows, cols), F32))
        swapped = jnp.concatenate(parts, axis=0)
        ci = (2.0 * m.astype(F32) - swapped).astype(BF16)
        acc = jnp.dot(m, W[0], preferred_element_type=F32)
        acc = acc + jnp.dot(ci, W[1], preferred_element_type=F32)
        acc = acc.astype(BF16)

        @pl.when(t == nc - 1)
        def _():
            T[c] = acc

        @pl.when(t < nc - 1)
        def _():
            O[t] = acc
            out_copy(t, chip, c).start()

        return carry

    lax.fori_loop(0, nc, step, 0)

    def line_copy(src, way, tile_at, there):
        return pltpu.make_async_remote_copy(
            src_ref=src, dst_ref=R.at[way, tile_at],
            send_sem=lsem.at[way, tile_at], recv_sem=lrx.at[way, tile_at],
            device_id={"occ": o, "vir": there}, device_id_type=MESH,
        )

    def plane_wait(at):
        @pl.when(c != at)
        def _():
            out_copy(0, c, at).wait_recv()

    for zz in range(nv):

        @pl.when(z == zz)
        def _():
            ups = [(q, 0) for q in range(nv - 1, zz, -1)]
            downs = [(q, 1) for q in range(zz)]
            order = ups + downs if 2 * zz < nv else downs + ups
            started = []
            for q, way in order:
                there = zz + 1 if way == 0 else zz - 1
                first = zz == 0 if way == 0 else zz == nv - 1
                plane_wait(q)
                if first:
                    src = T.at[q]
                else:
                    src = R.at[way, q]
                    line_copy(src, way, q, there).wait_recv()
                    R[way, q] = (R[way, q].astype(F32) + T[q].astype(F32)).astype(BF16)
                d = line_copy(src, way, q, there)
                d.start()
                started.append(d)
            plane_wait(zz)
            total = T[zz].astype(F32)
            for way, any_in in ((0, zz > 0), (1, zz < nv - 1)):
                if any_in:
                    line_copy(R.at[way, zz], way, zz, zz + 1 if zz == 0 else zz - 1).wait_recv()
                    total = total + R[way, zz].astype(F32)
            out[...] = (keep_ref[...] * total[:rows]).astype(BF16)
            for d in started:
                d.wait_send()

    for d in sends:
        d.wait_send()
    for t in range(nc - 1):
        out_copy(t, c, c).wait_send()


def fused(amplitudes, ladder_ints, cycle_ints, screen):
    norb, tiles = screen.shape
    rows, cols = amplitudes.shape
    nocc = rows // norb
    nv = lax.axis_size("vir")
    groups = lax.axis_size("occ")
    pad = -(-rows // 16) * 16
    vmem = pl.BlockSpec(memory_space=pltpu.VMEM)
    return pl.pallas_call(
        functools.partial(kernel, nv, norb, nocc),
        out_shape=jax.ShapeDtypeStruct((rows, cols), BF16),
        in_specs=[vmem] * 4,
        out_specs=vmem,
        scratch_shapes=[
            pltpu.VMEM((groups, pad, cols), BF16),
            pltpu.VMEM((cols // LANES, groups * rows, LANES), F32),
            pltpu.VMEM((2, 2) + ladder_ints.shape, BF16),
            pltpu.VMEM((2, cols, cols), BF16),
            pltpu.VMEM((nv - 1, pad, cols), BF16),
            pltpu.VMEM((nv, pad, cols), BF16),
            pltpu.VMEM((2, nv, pad, cols), BF16),
            pltpu.VMEM((rows, cols), F32),
            pltpu.SemaphoreType.DMA((12,)),
            pltpu.SemaphoreType.DMA((12,)),
            pltpu.SemaphoreType.DMA((nv - 1,)),
            pltpu.SemaphoreType.DMA((nv,)),
            pltpu.SemaphoreType.DMA((2, nv)),
            pltpu.SemaphoreType.DMA((2, nv)),
        ],
        compiler_params=pltpu.CompilerParams(
            collective_id=0, has_side_effects=True, vmem_limit_bytes=48 * 2**20
        ),
    )(amplitudes, ladder_ints, cycle_ints, screen)


def shards(amplitudes, ladder_ints, cycle_ints, screen):
    groups, planes = lax.axis_size("occ"), lax.axis_size("vir")
    rows, cols = amplitudes.shape
    fits = (
        groups == 2 * planes
        and planes == 4
        and cols == 2 * ladder_ints.shape[1]
        and cols == ladder_ints.shape[0]
        and cols % LANES == 0
        and (rows // screen.shape[0]) % 8 == 0
        and groups * rows * cols * 6 < 24 * 2**20
    )
    return (fused if fits else plain)(amplitudes, ladder_ints, cycle_ints, screen)


def solution(mesh):
    placed = (P("occ", "vir"), P("vir", "occ"), P("vir", "occ"), P("occ", "vir"))
    return jax.shard_map(
        shards, mesh=mesh, in_specs=placed, out_specs=P("occ", "vir"), check_vma=False
    )
```

```python
import functools

import jax
import jax.numpy as jnp
from jax import lax
from jax.experimental import pallas as pl
from jax.experimental.pallas import tpu as pltpu
from jax.sharding import PartitionSpec as P

MESH = pl.DeviceIdType.MESH
LANES = 128
F32, BF16 = jnp.float32, jnp.bfloat16


def plain(amplitudes, ladder_ints, cycle_ints, screen):
    orbital_rows, tile_count = screen.shape
    occupied = amplitudes.shape[0] // orbital_rows
    columns = amplitudes.shape[1]
    tile_width = columns // tile_count
    groups = lax.axis_size("occ")
    values = screen.astype(F32)
    keep = jnp.broadcast_to(
        values[:, None, :, None], (orbital_rows, occupied, tile_count, tile_width)
    )
    keep = keep.reshape(orbital_rows * occupied, columns)
    masked = (amplitudes.astype(F32) * keep).astype(BF16)
    blocks = masked.reshape(orbital_rows, groups, orbital_rows, columns)
    arrived = lax.all_to_all(blocks, "occ", split_axis=1, concat_axis=1, tiled=True)
    swapped = arrived.transpose(2, 1, 0, 3).reshape(orbital_rows * occupied, columns)
    cycle_input = (2.0 * masked.astype(F32) - swapped.astype(F32)).astype(BF16)
    cycle_part = jnp.dot(
        cycle_input,
        lax.all_gather(cycle_ints, "occ", axis=1, tiled=True),
        preferred_element_type=F32,
    )
    ladder = jnp.dot(
        masked,
        lax.all_gather(ladder_ints, "occ", axis=1, tiled=True),
        preferred_element_type=F32,
    )
    summed = lax.psum_scatter(ladder + cycle_part, "vir", scatter_dimension=1, tiled=True)
    return (keep * summed).astype(BF16)


def ordinal(x, width, count):
    return sum((x >= width * n).astype(jnp.int32) for n in range(1, count))


def one_hot(target, width):
    lanes = lax.broadcasted_iota(jnp.int32, (target.shape[0], width), 1)
    return (lanes == target).astype(F32).astype(BF16)


def kernel(
    nv, norb, nocc,
    amp, lad, cyc, scr, out,
    G, I, W, O, T, R, F, keep_ref,
    gs, gr, osem, orx, lsem, lrx,
):
    rows, cols = out.shape
    groups, pad = G.shape[:2]
    half = cols // 2
    tile = cols // scr.shape[1]
    q4 = groups // 2
    jh = nocc // 2
    hr = rows // 2
    low = (hr // 16) * 16
    high = -(-hr // 16) * 16
    spans = ((0, low), (low, pad - low))
    gather = ((0, high), (high, pad - high))
    mid = -(-high // 32) * 16
    mid2 = high + -(-(pad - high) // 32) * 16
    subs = ((0, mid), (mid, high - mid), (high, mid2 - high), (mid2, pad - mid2))
    o = lax.axis_index("occ")
    z = lax.axis_index("vir")
    k = o % 2
    c = o // 2
    nc = nv
    sib = o + 1 - 2 * k
    cx = c + 1 - 2 * (c % 2)
    cy = c + 2 - 4 * ((c // 2) % 2)
    cd = cx + 2 - 4 * ((cx // 2) % 2)
    X, Y, D = 2 * cx + k, 2 * cy + k, 2 * cd + k

    barrier = pltpu.get_barrier_semaphore()
    for p in (sib, X, Y, D):
        pl.semaphore_signal(barrier, inc=1, device_id={"occ": p, "vir": z}, device_id_type=MESH)
    for there, ok in ((z - 1, z > 0), (z + 1, z < nv - 1)):

        @pl.when(ok)
        def _():
            pl.semaphore_signal(
                barrier, inc=1, device_id={"occ": o, "vir": there}, device_id_type=MESH
            )

    t_of = lax.broadcasted_iota(jnp.int32, (scr.shape[1], cols), 0)
    v_of = lax.broadcasted_iota(jnp.int32, (scr.shape[1], cols), 1)
    spread = ((v_of >= t_of * tile) & (v_of < (t_of + 1) * tile)).astype(F32)
    wide = jnp.dot(scr[...].astype(F32), spread, preferred_element_type=F32)
    r_of = lax.broadcasted_iota(jnp.int32, (rows, norb), 0)
    a_of = lax.broadcasted_iota(jnp.int32, (rows, norb), 1)
    pick = ((r_of >= a_of * nocc) & (r_of < (a_of + 1) * nocc)).astype(F32)
    keep = jnp.dot(pick, wide, preferred_element_type=F32)
    keep_ref[...] = keep
    masked = (amp[...].astype(F32) * keep).astype(BF16)

    side = o // q4
    r = lax.broadcasted_iota(jnp.int32, (pad, 1), 0)
    cl = ordinal(r, hr, 2)
    rr = r - cl * hr
    a = ordinal(rr, jh, norb)
    source = a * nocc + (cl + side - 2 * cl * side) * jh + rr - a * jh
    source = jnp.where(r < rows, source, -1)
    G[o] = jnp.dot(one_hot(source, rows), masked, preferred_element_type=F32).astype(BF16)

    pl.semaphore_wait(barrier, jnp.where((z == 0) | (z == nv - 1), 5, 6))

    def cp(src, dst, sem, p):
        return pltpu.make_async_remote_copy(
            src_ref=src, dst_ref=dst, send_sem=gs.at[sem], recv_sem=gr.at[sem],
            device_id={"occ": p, "vir": z}, device_id_type=MESH,
        )

    sends = []

    def send(s, span, sem, p):
        ref = G.at[s, pl.ds(*span)]
        d = cp(ref, ref, sem, p)
        d.start()
        sends.append(d)

    def arrive(s, span, sem):
        ref = G.at[s, pl.ds(*span)]
        cp(ref, ref, sem, sib).wait_recv()

    SX, SY, SD = X + 1 - 2 * k, Y + 1 - 2 * k, D + 1 - 2 * k

    def own_out(n):
        e, f = subs[2 * n], subs[2 * n + 1]
        b = 10 * n
        send(o, e, b + 0, X)
        send(o, f, b + 3, Y)
        send(o, f, b + 1, X)
        send(o, e, b + 2, Y)
        send(o, gather[n], b + 6, sib)

    def forward(n):
        e, f = subs[2 * n], subs[2 * n + 1]
        b = 10 * n
        arrive(X, e, b + 0)
        send(X, e, b + 4, Y)
        arrive(Y, f, b + 3)
        send(Y, f, b + 5, X)

    def collect(n):
        e, f = subs[2 * n], subs[2 * n + 1]
        b = 10 * n
        arrive(X, f, b + 1)
        send(X, gather[n], b + 7, sib)
        arrive(Y, e, b + 2)
        send(Y, gather[n], b + 8, sib)

    def finish(n):
        e, f = subs[2 * n], subs[2 * n + 1]
        b = 10 * n
        arrive(sib, gather[n], b + 6)
        arrive(D, e, b + 4)
        arrive(D, f, b + 5)
        send(D, gather[n], b + 9, sib)
        arrive(SX, gather[n], b + 7)
        arrive(SY, gather[n], b + 8)
        arrive(SD, gather[n], b + 9)

    own_out(0)
    for m, ref in enumerate((lad, cyc)):
        d = cp(ref, I.at[k, m], 20 + m, sib)
        d.start()
        sends.append(d)
        I[k, m] = ref[...]
    forward(0)
    own_out(1)
    collect(0)
    for m in range(2):
        cp(I.at[1 - k, m], I.at[1 - k, m], 20 + m, sib).wait_recv()
        W[m] = jnp.concatenate([I[0, m], I[1, m]], axis=1)
    finish(0)

    def out_copy(n, t, chip, slot):
        return pltpu.make_async_remote_copy(
            src_ref=O.at[t, pl.ds(*spans[n])], dst_ref=T.at[slot, pl.ds(*spans[n])],
            send_sem=osem.at[n, t], recv_sem=orx.at[n, slot],
            device_id={"occ": 2 * chip + k, "vir": z}, device_id_type=MESH,
        )

    def compute(n):
        at, size = spans[n]
        r = at + lax.broadcasted_iota(jnp.int32, (size, 1), 0)
        cl = ordinal(r, hr, 2)
        rr = r - cl * hr
        a = ordinal(rr, jh, norb)
        jj = rr - a * jh
        sd = ordinal(jj, norb, q4)
        row = (jj - sd * norb) * jh + a
        if n == 0:
            base = sd * high + row
            width = q4 * high
        else:
            base = jnp.where(cl == 0, q4 * size + row, sd * size + hr - at + row)
            base = jnp.where(r < rows, base, -groups * pad)
            width = q4 * size + high

        def step(t, carry):
            chip = (c + t + 1) % nc
            dest = 2 * chip + k
            there = dest // q4
            m = G[dest, pl.ds(at, size)]
            if n == 0:
                pool = [G[there * q4 + s, pl.ds(0, high)] for s in range(q4)]
            else:
                pool = [G[(1 - there) * q4 + s, pl.ds(at, size)] for s in range(q4)]
                pool.append(G[there * q4 + q4 - 1, pl.ds(0, high)])
            pool = jnp.concatenate(pool, axis=0)
            perm = one_hot(base + (dest % q4) * norb, width)
            swapped = jnp.dot(perm, pool, preferred_element_type=F32)
            ci = (2.0 * m.astype(F32) - swapped).astype(BF16)
            acc = jnp.dot(m, W[0], preferred_element_type=F32)
            acc = acc + jnp.dot(ci, W[1], preferred_element_type=F32)
            acc = acc.astype(BF16)

            @pl.when(t == nc - 1)
            def _():
                T[c, pl.ds(at, size)] = acc

            @pl.when(t < nc - 1)
            def _():
                O[t, pl.ds(at, size)] = acc
                out_copy(n, t, chip, c).start()

            return carry

        lax.fori_loop(0, nc, step, 0)

    forward(1)
    compute(0)
    collect(1)
    finish(1)
    compute(1)

    def line_copy(n, src, way, tile_at, there):
        return pltpu.make_async_remote_copy(
            src_ref=src.at[pl.ds(*spans[n])], dst_ref=R.at[way, tile_at, pl.ds(*spans[n])],
            send_sem=lsem.at[n, way, tile_at], recv_sem=lrx.at[n, way, tile_at],
            device_id={"occ": o, "vir": there}, device_id_type=MESH,
        )

    def plane_wait(n, at):
        @pl.when(c != at)
        def _():
            out_copy(n, 0, c, at).wait_recv()

    for zz in range(nv):

        @pl.when(z == zz)
        def _():
            ups = [(q, 0) for q in range(nv - 1, zz, -1)]
            downs = [(q, 1) for q in range(zz)]
            order = ups + downs if 2 * zz < nv else downs + ups
            started = []
            for n in range(2):
                span = pl.ds(*spans[n])
                for q, way in order:
                    there = zz + 1 if way == 0 else zz - 1
                    first = zz == 0 if way == 0 else zz == nv - 1
                    plane_wait(n, q)
                    if first:
                        src = T.at[q]
                    else:
                        src = R.at[way, q]
                        line_copy(n, src, way, q, there).wait_recv()
                        R[way, q, span] = (
                            R[way, q, span].astype(F32) + T[q, span].astype(F32)
                        ).astype(BF16)
                    d = line_copy(n, src, way, q, there)
                    d.start()
                    started.append(d)
            for n in range(2):
                span = pl.ds(*spans[n])
                plane_wait(n, zz)
                total = T[zz, span].astype(F32)
                for way, any_in in ((0, zz > 0), (1, zz < nv - 1)):
                    if any_in:
                        line_copy(
                            n, R.at[way, zz], way, zz, zz + 1 if zz == 0 else zz - 1
                        ).wait_recv()
                        total = total + R[way, zz, span].astype(F32)
                F[span] = total.astype(BF16)
            for d in started:
                d.wait_send()

    r = lax.broadcasted_iota(jnp.int32, (rows, 1), 0)
    a = ordinal(r, nocc, norb)
    j = r - a * nocc
    jside = ordinal(j, jh, 2)
    cl = jside + side - 2 * jside * side
    place = cl * hr + a * jh + j - jside * jh
    back = jnp.dot(one_hot(place, pad), F[...], preferred_element_type=F32)
    out[...] = (keep_ref[...] * back).astype(BF16)

    for d in sends:
        d.wait_send()
    for n in range(2):
        for t in range(nc - 1):
            out_copy(n, t, c, c).wait_send()


def fused(amplitudes, ladder_ints, cycle_ints, screen):
    norb, tiles = screen.shape
    rows, cols = amplitudes.shape
    nocc = rows // norb
    nv = lax.axis_size("vir")
    groups = lax.axis_size("occ")
    pad = -(-rows // 16) * 16
    vmem = pl.BlockSpec(memory_space=pltpu.VMEM)
    return pl.pallas_call(
        functools.partial(kernel, nv, norb, nocc),
        out_shape=jax.ShapeDtypeStruct((rows, cols), BF16),
        in_specs=[vmem] * 4,
        out_specs=vmem,
        scratch_shapes=[
            pltpu.VMEM((groups, pad, cols), BF16),
            pltpu.VMEM((2, 2) + ladder_ints.shape, BF16),
            pltpu.VMEM((2, cols, cols), BF16),
            pltpu.VMEM((nv - 1, pad, cols), BF16),
            pltpu.VMEM((nv, pad, cols), BF16),
            pltpu.VMEM((2, nv, pad, cols), BF16),
            pltpu.VMEM((pad, cols), BF16),
            pltpu.VMEM((rows, cols), F32),
            pltpu.SemaphoreType.DMA((22,)),
            pltpu.SemaphoreType.DMA((22,)),
            pltpu.SemaphoreType.DMA((2, nv - 1)),
            pltpu.SemaphoreType.DMA((2, nv)),
            pltpu.SemaphoreType.DMA((2, 2, nv)),
            pltpu.SemaphoreType.DMA((2, 2, nv)),
        ],
        compiler_params=pltpu.CompilerParams(
            collective_id=0, has_side_effects=True, vmem_limit_bytes=48 * 2**20
        ),
    )(amplitudes, ladder_ints, cycle_ints, screen)


def shards(amplitudes, ladder_ints, cycle_ints, screen):
    groups, planes = lax.axis_size("occ"), lax.axis_size("vir")
    rows, cols = amplitudes.shape
    fits = (
        groups == 2 * planes
        and planes == 4
        and cols == 2 * ladder_ints.shape[1]
        and cols == ladder_ints.shape[0]
        and cols % LANES == 0
        and rows % 16 == 8
        and rows // screen.shape[0] == groups * screen.shape[0]
        and (rows // 2) % 16 <= screen.shape[0]
        and groups * rows * cols * 2 < 16 * 2**20
    )
    return (fused if fits else plain)(amplitudes, ladder_ints, cycle_ints, screen)


def solution(mesh):
    placed = (P("occ", "vir"), P("vir", "occ"), P("vir", "occ"), P("occ", "vir"))
    return jax.shard_map(
        shards, mesh=mesh, in_specs=placed, out_specs=P("occ", "vir"), check_vma=False
    )
```
